512 devices in a mesh: row: 32 (over z_hi, y, core), col: 16 (over z_lo, x).
Axes of the slice: x: 4, y: 4, z: 16 (z_hi: 4, z_lo: 4; z = z_hi * 4 + z_lo), core: 2. Of those that a mesh axis runs over, the one named last changes fastest.
Arguments:
- star_phase: float32 [9, 65536], P(None, ('row', 'col')), may hold values from -6 to 6
- star_mass: float32 [65536], P(('row', 'col')), may hold values from 0.25 to 4
- due_mask: int32 [65536], P(('row', 'col')), may hold values 0 or 1
Outputs:
- derivatives: float32 [9, 65536], P(None, ('row', 'col'))
The draws below stay inside these ranges and needn't reach their ends.
Inputs may be any that keep to these rules, and one draw needn't show every extreme that they name: `due_mask`: 1 marks a due star.
All inputs are finite; a program needn't handle non-finite values. No bound on the sum of `due_mask` on one device may be relied on, other than what follows from the above.
Results may differ from the reference program's by a relative error of at most 0.00016.
Values sent between devices are 32-bit elements; how exact they have to be, the bound alone decides.
No kernel may reach another device: no remote copies, remote signals or barrier semaphores. Data moves between devices by JAX's collectives and lax.ppermute only.
A program may use at most 64 MiB of HBM per device.

```python
import math
import jax
import jax.numpy as jnp
from jax import lax

STARS = 65536


def touch_ends(drawn, key, least, high):
    shape = drawn.shape
    place = [jax.random.randint(jax.random.fold_in(key, axis), (), 0, shape[axis]) for axis in range(len(shape))]
    drawn = drawn.at[tuple(place)].set(least)
    longest = shape.index(max(shape))
    place[longest] = (place[longest] + 1) % shape[longest]
    return drawn.at[tuple(place)].set(high)


def block_scale(rng, dims, cuts, low, high):
    gain = 1.0
    for axis_at, blocks in cuts:
        steps = jax.random.uniform(jax.random.fold_in(jax.random.fold_in(rng, 6), axis_at), (blocks,), jnp.float32, low / len(cuts), high / len(cuts))
        gain = gain * jnp.repeat(jnp.exp(steps), dims[axis_at] // blocks).reshape((-1,) + (1,) * (len(dims) - 1 - axis_at))
    return gain


def bell_draw(rng, shape, scale, most, shards=(), dtype=jnp.bfloat16):
    array = scale * jax.random.normal(rng, shape, jnp.float32)
    if shards:
        array = array * block_scale(rng, shape, shards, -0.22, 0.18)
    return jnp.clip(array, -most, most).astype(dtype)


def setup_inputs(seed: int = 0) -> dict:
    key_of = jax.random.split(jax.random.key(seed), 4)
    return {
        "star_phase": bell_draw(key_of[0], (9, STARS), 1.0, 6.0, ((1, 512),), jnp.float32),
        "star_mass": jnp.clip(jnp.exp(math.log(4.0) - 2.7725887 * jax.random.uniform(key_of[1], (STARS,), jnp.float32) ** block_scale(key_of[1], (STARS,), ((0, 512),), -0.2, 0.2)), 0.25, 4.0),
        "due_mask": touch_ends((jax.random.randint(key_of[2], (STARS,), 0, 4) < 3).astype(jnp.int32), jax.random.fold_in(key_of[2], 1), 0, 1),
    }


softening = 0.01

def pair_field(targets, sources):
    deltas = [sources[component][None, :] - targets[component][:, None] for component in range(9)]
    spread = deltas[0] * deltas[0] + deltas[1] * deltas[1] + deltas[2] * deltas[2] + softening
    reciprocal = lax.rsqrt(spread)
    recip_square = reciprocal * reciprocal
    recip_cube = reciprocal * recip_square
    radial_rate = (deltas[0] * deltas[3] + deltas[1] * deltas[4] + deltas[2] * deltas[5]) * recip_square
    second_rate = (deltas[3] * deltas[3] + deltas[4] * deltas[4] + deltas[5] * deltas[5] + deltas[0] * deltas[6] + deltas[1] * deltas[7] + deltas[2] * deltas[8]) * recip_square
    second_rate = second_rate + radial_rate * radial_rate
    accel = [deltas[component] * recip_cube for component in range(3)]
    jerk_part = [deltas[component + 3] * recip_cube - 3.0 * radial_rate * accel[component] for component in range(3)]
    snap_part = [deltas[component + 6] * recip_cube - 6.0 * radial_rate * jerk_part[component] - 3.0 * second_rate * accel[component] for component in range(3)]
    return accel + jerk_part + snap_part

def reference(star_phase, star_mass, due_mask):
    width = min(256, STARS)
    blocks = star_phase.reshape(9, STARS // width, width).transpose(1, 0, 2)

    def one_block(target_rows):
        fields = pair_field(target_rows, star_phase)
        return jnp.stack([lax.optimization_barrier(jnp.sum(field_term * star_mass[None, :], axis=1)) for field_term in fields])
    sums = lax.map(one_block, blocks)
    sums = sums.transpose(1, 0, 2).reshape(9, STARS)
    return sums / jnp.float32(STARS) * due_mask.astype(jnp.float32)[None, :]
```

```python
import functools

import jax
import jax.numpy as jnp
from jax import lax
from jax.experimental import pallas as pl
from jax.experimental.pallas import tpu as pltpu
from jax.sharding import PartitionSpec as P

F32 = jnp.float32
BF16 = jnp.bfloat16
SOFTENING = 0.01
LANES = 128
WIDE = 4
COMBOS = ("hh", "hm", "mh", "mm", "hl", "lh")


def split3(value):
    high = value.astype(BF16)
    rest = value - high.astype(F32)
    middle = rest.astype(BF16)
    low = (rest - middle.astype(F32)).astype(BF16)
    return {"h": high, "m": middle, "l": low}


def dot(left, right):
    return jnp.dot(left, right, preferred_element_type=F32)


def pair_kernel(
    tile_i, tile_j, targets, sources, out, stage, left_rate, left_second,
    right_rate, right_second, feat_c, feat_p, feat_u, place, totals
):
    target_blocks, source_blocks = targets.shape[0], sources.shape[0]
    target_count, source_count = target_blocks * LANES, source_blocks * LANES
    width = WIDE * LANES

    def rows(ref, block, low, high):
        return jnp.concatenate([ref[block * WIDE + k, low:high, :] for k in range(WIDE)], axis=1)

    def put(pieces, height):
        stage[0:height, :] = jnp.zeros((height, width), F32)
        for at, piece in pieces:
            stage[at : at + piece.shape[0], :] = piece
        return split3(stage[0:height, :])

    one = jnp.ones((1, width), F32)

    def prepare_sources(block, carry):
        lanes = pl.ds(pl.multiple_of(block * width, width), width)
        x, v, a = (rows(sources, block, k, k + 3) for k in (0, 3, 6))
        m = rows(sources, block, 9, 10)
        x_v = jnp.sum(x * v, axis=0, keepdims=True)
        second = jnp.sum(v * v + x * a, axis=0, keepdims=True)
        parts = put([(0, v), (3, x), (6, one), (7, x_v)], 16)
        right_rate[:, lanes] = jnp.concatenate([parts[c[1]] for c in COMBOS], axis=0)
        parts = put([(0, 0.2 * v), (3, 0.2 * a), (6, 0.2 * x), (9, one), (10, 0.2 * second)], 16)
        right_second[:, lanes] = jnp.concatenate([parts[c[1]] for c in COMBOS], axis=0)
        empty = jnp.zeros((32, width), F32)
        mx, mv = m * x, m * v
        for ref, pieces in (
            (feat_c, [(0, m), (1, mx), (4, mv), (7, m * a)]),
            (feat_p, [(10, m), (11, mx), (14, mv)]),
            (feat_u, [(17, m), (18, mx)]),
        ):
            parts = put(pieces, 32)
            tall = jnp.concatenate([parts[k].astype(F32) for k in "hml"] + [empty], axis=0)
            ref[lanes, :] = tall.T.astype(BF16)
        return carry

    def prepare_targets(block, carry):
        lanes = pl.ds(pl.multiple_of(block * width, width), width)
        x, v, a = (rows(targets, block, k, k + 3) for k in (0, 3, 6))
        x_v = jnp.sum(x * v, axis=0, keepdims=True)
        second = jnp.sum(v * v + x * a, axis=0, keepdims=True)
        empty = jnp.zeros((32, width), F32)
        for ref, pieces in (
            (left_rate, [(0, -x), (3, -v), (6, x_v), (7, one)]),
            (left_second, [(0, -2.0 * v), (3, -x), (6, -a), (9, 0.2 * second), (10, one)]),
        ):
            parts = put(pieces, 16)
            tall = jnp.concatenate([parts[c[0]].astype(F32) for c in COMBOS] + [empty], axis=0)
            ref[lanes, :] = tall.T.astype(BF16)
        for k in range(3):
            place[k, lanes, :] = jnp.broadcast_to(x[k : k + 1, :], (LANES, width)).T
        return carry

    lax.fori_loop(0, source_blocks // WIDE, prepare_sources, 0)
    lax.fori_loop(0, target_blocks // WIDE, prepare_targets, 0)
    totals[...] = jnp.zeros_like(totals)

    def column(block, carry):
        js = pl.ds(pl.multiple_of(block * tile_j, tile_j), tile_j)
        xs=[jnp.concatenate([sources[block*(tile_j//LANES)+q,k:k+1,:] for q in range(tile_j//LANES)],axis=1) for k in range(3)]
        for turn in range(target_count // tile_i):
            is_ = pl.ds(turn * tile_i, tile_i)
            rate = dot(left_rate[is_, 0:96], right_rate[:, js])
            second = dot(left_second[is_, 0:96], right_second[:, js])
            spread = None
            for k in range(3):
                here = jnp.concatenate([place[k, is_, :]] * (tile_j // LANES), axis=1)
                delta = xs[k] - here
                spread = delta * delta + SOFTENING if spread is None else spread + delta * delta
            recip = lax.rsqrt(spread)
            square = recip * recip
            cube = recip * square
            p = rate * square
            added = None
            for weight, feat in (
                (cube, feat_c), (p * cube, feat_p), ((p * p - second * square) * cube, feat_u)
            ):
                high = weight.astype(BF16)
                low = (weight - high.astype(F32)).astype(BF16)
                part = dot(high, feat[js, :]) + dot(low, feat[js, :])
                added = part if added is None else added + part
            totals[is_, :] += added
        return carry

    lax.fori_loop(0, source_count // tile_j, column, 0)

    def finish(block, carry):
        t = totals[pl.ds(pl.multiple_of(block * LANES, LANES), LANES), :].T
        t = t[0:32] + t[32:64] + t[64:96]
        x, v, a = (targets[block, k : k + 3, :] for k in (0, 3, 6))
        out[block, 0:3, :] = t[1:4] - x * t[0:1]
        out[block, 3:6, :] = t[4:7] - v * t[0:1] - 3.0 * (t[11:14] - x * t[10:11])
        out[block, 6:9, :] = (
            t[7:10] - a * t[0:1] - 6.0 * (t[14:17] - v * t[10:11]) + 15.0 * (t[18:21] - x * t[17:18])
        )
        return carry

    lax.fori_loop(0, target_blocks, finish, 0)


def pair_sums(targets, sources, tile_i=256, tile_j=256):
    target_count, source_count = targets.shape[0] * LANES, sources.shape[0] * LANES
    return pl.pallas_call(
        functools.partial(pair_kernel, tile_i, tile_j),
        out_shape=jax.ShapeDtypeStruct((targets.shape[0], 9, LANES), F32),
        in_specs=[pl.BlockSpec(memory_space=pltpu.VMEM)] * 2,
        out_specs=pl.BlockSpec(memory_space=pltpu.VMEM),
        scratch_shapes=[
            pltpu.VMEM((32, WIDE * LANES), F32),
            pltpu.VMEM((target_count, LANES), BF16),
            pltpu.VMEM((target_count, LANES), BF16),
            pltpu.VMEM((96, source_count), BF16),
            pltpu.VMEM((96, source_count), BF16),
            pltpu.VMEM((source_count, LANES), BF16),
            pltpu.VMEM((source_count, LANES), BF16),
            pltpu.VMEM((source_count, LANES), BF16),
            pltpu.VMEM((3, target_count, LANES), F32),
            pltpu.VMEM((target_count, LANES), F32),
        ],
        compiler_params=pltpu.CompilerParams(vmem_limit_bytes=56 * 2**20),
        name="pair_sums",
    )(targets, sources)


def gathered(block, axis):
    count = lax.axis_size(axis)
    copies = jnp.broadcast_to(block[None], (count,) + block.shape)
    return lax.all_to_all(copies, axis, 0, 0, tiled=True)


def on_device(star_phase, star_mass, due_mask):
    stars = jnp.concatenate(
        [star_phase, star_mass[None, :], jnp.zeros((6, star_mass.shape[0]), F32)], axis=0
    )
    targets = gathered(stars, "col")
    sources = gathered(stars, "row")
    sums = pair_sums(targets, sources)
    mine = jnp.sum(lax.all_to_all(sums, "col", 0, 0, tiled=True), axis=0)
    total = star_mass.shape[0] * lax.axis_size("row") * lax.axis_size("col")
    return mine / jnp.float32(total) * due_mask.astype(F32)[None, :]


def solution(mesh):
    both = ("row", "col")
    return jax.shard_map(
        on_device, mesh=mesh, in_specs=(P(None, both), P(both), P(both)), out_specs=P(None, both), check_vma=False
    )
```

```python
import functools

import jax
import jax.numpy as jnp
from jax import lax
from jax.experimental import pallas as pl
from jax.experimental.pallas import tpu as pltpu
from jax.sharding import PartitionSpec as P

F32 = jnp.float32
BF16 = jnp.bfloat16
SOFTENING = 0.01
LANES = 128
TARGET_TILE = 256
WIDE = 4
COMBOS = ("hh", "hm", "mh", "mm", "hl", "lh")


def split3(value):
    high = value.astype(BF16)
    rest = value - high.astype(F32)
    middle = rest.astype(BF16)
    low = (rest - middle.astype(F32)).astype(BF16)
    return {"h": high, "m": middle, "l": low}


def dot(left, right):
    return jnp.dot(left, right, preferred_element_type=F32)


def pair_kernel(
    tile, unroll, targets, sources, out, stage, left_rate, left_second,
    right_rate, right_second, feats, place, totals
):
    target_blocks, source_blocks = targets.shape[0], sources.shape[0]
    target_count, source_count = target_blocks * LANES, source_blocks * LANES
    width = WIDE * LANES

    def rows(ref, block, low, high):
        return jnp.concatenate([ref[block * WIDE + k, low:high, :] for k in range(WIDE)], axis=1)

    def put(pieces, height):
        stage[0:height, :] = jnp.zeros((height, width), F32)
        for at, piece in pieces:
            stage[at : at + piece.shape[0], :] = piece
        return split3(stage[0:height, :])

    one = jnp.ones((1, width), F32)

    def prepare_sources(block, carry):
        lanes = pl.ds(pl.multiple_of(block * width, width), width)
        x, v, a = (rows(sources, block, k, k + 3) for k in (0, 3, 6))
        m = rows(sources, block, 9, 10)
        x_v = jnp.sum(x * v, axis=0, keepdims=True)
        second = jnp.sum(v * v + x * a, axis=0, keepdims=True)
        empty = jnp.zeros((32, width), F32)
        for ref, pieces in (
            (right_rate, [(0, v), (3, x), (6, one), (7, x_v)]),
            (right_second, [(0, 0.2 * v), (3, 0.2 * a), (6, 0.2 * x), (9, one), (10, 0.2 * second)]),
        ):
            parts = put(pieces, 16)
            tall = jnp.concatenate([parts[c[1]].astype(F32) for c in COMBOS] + [empty], axis=0)
            ref[lanes, :] = tall.T.astype(BF16)
        for k in range(3):
            place[k, lanes, :] = jnp.broadcast_to(x[k : k + 1, :], (LANES, width)).T
        parts = put([(0, m), (1, m * x), (4, m * v), (7, m * a)], 16)
        stage[...] = jnp.zeros_like(stage)
        for k, name in enumerate("hml"):
            part = parts[name].astype(F32)
            stage[10 * k : 10 * k + 10, :] = part[0:10]
            stage[32 + 7 * k : 39 + 7 * k, :] = part[0:7]
            stage[64 + 4 * k : 68 + 4 * k, :] = part[0:4]
        feats[:, lanes] = stage[...].astype(BF16)
        return carry

    def prepare_targets(block, carry):
        lanes = pl.ds(pl.multiple_of(block * width, width), width)
        x, v, a = (rows(targets, block, k, k + 3) for k in (0, 3, 6))
        x_v = jnp.sum(x * v, axis=0, keepdims=True)
        second = jnp.sum(v * v + x * a, axis=0, keepdims=True)
        for ref, pieces in (
            (left_rate, [(0, -x), (3, -v), (6, x_v), (7, one)]),
            (left_second, [(0, -2.0 * v), (3, -x), (6, -a), (9, 0.2 * second), (10, one)]),
        ):
            parts = put(pieces, 16)
            ref[:, lanes] = jnp.concatenate([parts[c[0]] for c in COMBOS], axis=0)
        return carry

    lax.fori_loop(0, source_blocks // WIDE, prepare_sources, 0)
    lax.fori_loop(0, target_blocks // WIDE, prepare_targets, 0)
    totals[...] = jnp.zeros_like(totals)
    turns = source_count // (tile * unroll)
    tb = TARGET_TILE // LANES

    def cell(step, carry):
        i_at, j_at = step // turns, step % turns
        lanes = pl.ds(pl.multiple_of(i_at * TARGET_TILE, TARGET_TILE), TARGET_TILE)
        xs=[jnp.concatenate([targets[i_at * tb + q, k : k + 1, :] for q in range(tb)],axis=1) for k in range(3)]
        sums = [None, None, None]
        for turn in range(unroll):
            js = pl.ds(pl.multiple_of((j_at * unroll + turn) * tile, tile), tile)
            rate = dot(right_rate[js, 0:96], left_rate[:, lanes])
            second = dot(right_second[js, 0:96], left_second[:, lanes])
            spread = None
            for k in range(3):
                there = jnp.concatenate([place[k, js, :]] * tb, axis=1)
                delta = there - xs[k]
                spread = delta * delta + SOFTENING if spread is None else spread + delta * delta
            recip = lax.rsqrt(spread)
            square = recip * recip
            cube = recip * square
            p = rate * square
            weights = (cube, p * cube, (p * p - second * square) * cube)
            for k, weight in enumerate(weights):
                high = weight.astype(BF16)
                low = (weight - high.astype(F32)).astype(BF16)
                feat = feats[32 * k : min(32 * k + 32, 80), js]
                part = dot(feat, high) + dot(feat, low)
                sums[k] = part if sums[k] is None else sums[k] + part
        totals[:, lanes] += jnp.concatenate(sums, axis=0)
        return carry

    lax.fori_loop(0, (target_count // TARGET_TILE) * turns, cell, 0)

    def finish(block, carry):
        t = totals[:, pl.ds(pl.multiple_of(block * LANES, LANES), LANES)]
        c = t[0:10] + t[10:20] + t[20:30]
        p = t[32:39] + t[39:46] + t[46:53]
        u = t[64:68] + t[68:72] + t[72:76]
        x, v, a = (targets[block, k : k + 3, :] for k in (0, 3, 6))
        out[block, 0:3, :] = c[1:4] - x * c[0:1]
        out[block, 3:6, :] = c[4:7] - v * c[0:1] - 3.0 * (p[1:4] - x * p[0:1])
        out[block, 6:9, :] = (
            c[7:10] - a * c[0:1] - 6.0 * (p[4:7] - v * p[0:1]) + 15.0 * (u[1:4] - x * u[0:1])
        )
        return carry

    lax.fori_loop(0, target_blocks, finish, 0)


def pair_sums(targets, sources, tile=256, unroll=8):
    target_count, source_count = targets.shape[0] * LANES, sources.shape[0] * LANES
    return pl.pallas_call(
        functools.partial(pair_kernel, tile, unroll),
        out_shape=jax.ShapeDtypeStruct((targets.shape[0], 9, LANES), F32),
        in_specs=[pl.BlockSpec(memory_space=pltpu.VMEM)] * 2,
        out_specs=pl.BlockSpec(memory_space=pltpu.VMEM),
        scratch_shapes=[
            pltpu.VMEM((80, WIDE * LANES), F32),
            pltpu.VMEM((96, target_count), BF16),
            pltpu.VMEM((96, target_count), BF16),
            pltpu.VMEM((source_count, LANES), BF16),
            pltpu.VMEM((source_count, LANES), BF16),
            pltpu.VMEM((80, source_count), BF16),
            pltpu.VMEM((3, source_count, LANES), F32),
            pltpu.VMEM((80, target_count), F32),
        ],
        compiler_params=pltpu.CompilerParams(vmem_limit_bytes=56 * 2**20),
        name="pair_sums",
    )(targets, sources)


AXES = ("row", "col")


def device_groups(rows, cols):
    planes, lines = {}, {}
    for row in range(rows):
        for col in range(cols):
            z_hi, inner = row // 8, row % 8
            z_lo, x = col // 4, col % 4
            planes.setdefault((z_hi, z_lo), []).append(row * cols + col)
            lines.setdefault((inner, x), []).append(row * cols + col)
    return list(planes.values()), list(lines.values())


def exchange(blocks, groups):
    return lax.all_to_all(blocks, AXES, 0, 0, axis_index_groups=groups, tiled=True)


def gathered(block, groups):
    return exchange(jnp.broadcast_to(block[None], (len(groups[0]),) + block.shape), groups)


def on_device(star_phase, star_mass, due_mask):
    rows, cols = lax.axis_size("row"), lax.axis_size("col")
    planes, lines = device_groups(rows, cols)
    stars = jnp.concatenate(
        [star_phase, star_mass[None, :], jnp.zeros((6, star_mass.shape[0]), F32)], axis=0
    )
    targets = gathered(stars, planes)
    sources = gathered(stars, lines)
    sums = pair_sums(targets, sources)
    mine = jnp.sum(exchange(sums, planes), axis=0)
    total = star_mass.shape[0] * rows * cols
    return mine / jnp.float32(total) * due_mask.astype(F32)[None, :]


def solution(mesh):
    return jax.shard_map(
        on_device, mesh=mesh, in_specs=(P(None, AXES), P(AXES), P(AXES)), out_specs=P(None, AXES), check_vma=False
    )
```

```python
import functools

import jax
import jax.numpy as jnp
from jax import lax
from jax.experimental import pallas as pl
from jax.experimental.pallas import tpu as pltpu
from jax.sharding import PartitionSpec as P

F32 = jnp.float32
BF16 = jnp.bfloat16
SOFTENING = 0.01
LANES = 128
TARGET_TILE = 256
WIDE = 4
DUE = 10
COMBOS = ("hh", "hm", "mh", "mm", "hl", "lh")


def split3(value):
    high = value.astype(BF16)
    rest = value - high.astype(F32)
    middle = rest.astype(BF16)
    low = (rest - middle.astype(F32)).astype(BF16)
    return {"h": high, "m": middle, "l": low}


def dot(left, right):
    return jnp.dot(left, right, preferred_element_type=F32)


def pair_kernel(
    tile, unroll, targets, sources, out, stage, left_rate, left_second,
    right_rate, right_second, feats, place, totals, due, results, offsets
):
    target_blocks, source_blocks = targets.shape[0], sources.shape[0]
    target_count, source_count = target_blocks * LANES, source_blocks * LANES
    width = WIDE * LANES

    def rows(ref, block, low, high):
        return jnp.concatenate([ref[block * WIDE + k, low:high, :] for k in range(WIDE)], axis=1)

    def put(pieces, height):
        stage[0:height, :] = jnp.zeros((height, width), F32)
        for at, piece in pieces:
            stage[at : at + piece.shape[0], :] = piece
        return split3(stage[0:height, :])

    one = jnp.ones((1, width), F32)

    def prepare_sources(block, carry):
        lanes = pl.ds(pl.multiple_of(block * width, width), width)
        x, v, a = (rows(sources, block, k, k + 3) for k in (0, 3, 6))
        m = rows(sources, block, 9, 10)
        x_v = jnp.sum(x * v, axis=0, keepdims=True)
        second = jnp.sum(v * v + x * a, axis=0, keepdims=True)
        empty = jnp.zeros((32, width), F32)
        for ref, pieces in (
            (right_rate, [(0, v), (3, x), (6, one), (7, x_v)]),
            (right_second, [(0, 0.2 * v), (3, 0.2 * a), (6, 0.2 * x), (9, one), (10, 0.2 * second)]),
        ):
            parts = put(pieces, 16)
            tall = jnp.concatenate([parts[c[1]].astype(F32) for c in COMBOS] + [empty], axis=0)
            ref[lanes, :] = tall.T.astype(BF16)
        for k in range(3):
            place[k, lanes, :] = jnp.broadcast_to(x[k : k + 1, :], (LANES, width)).T
        parts = put([(0, m), (1, m * x), (4, m * v), (7, m * a)], 16)
        stage[...] = jnp.zeros_like(stage)
        for k, name in enumerate("hml"):
            part = parts[name].astype(F32)
            stage[10 * k : 10 * k + 10, :] = part[0:10]
            stage[32 + 7 * k : 39 + 7 * k, :] = part[0:7]
            stage[64 + 4 * k : 68 + 4 * k, :] = part[0:4]
        feats[:, lanes] = stage[...].astype(BF16)
        return carry

    lane = lax.broadcasted_iota(jnp.int32, (16, LANES), 1)
    counts = [jnp.sum(targets[k, DUE : DUE + 1, :]).astype(jnp.int32) for k in range(target_blocks)]
    offset = jnp.int32(0)
    for k in range(target_blocks):
        offsets[k] = offset
        offset = offset + counts[k]
    tiles = (offset + TARGET_TILE - 1) // TARGET_TILE
    due[...] = jnp.zeros_like(due)
    results[...] = jnp.zeros_like(results)

    def gather_due(block, carry):
        at, shift = offsets[block] // LANES, offsets[block] % LANES
        moved = pltpu.roll(targets[block], shift, 1)
        due[at] = jnp.where(lane >= shift, moved, due[at])
        due[at + 1] = moved
        return carry

    lax.fori_loop(0, target_blocks, gather_due, 0)

    def prepare_targets(block, carry):
        lanes = pl.ds(pl.multiple_of(block * width, width), width)
        x, v, a = (rows(due, block, k, k + 3) for k in (0, 3, 6))
        x_v = jnp.sum(x * v, axis=0, keepdims=True)
        second = jnp.sum(v * v + x * a, axis=0, keepdims=True)
        for ref, pieces in (
            (left_rate, [(0, -x), (3, -v), (6, x_v), (7, one)]),
            (left_second, [(0, -2.0 * v), (3, -x), (6, -a), (9, 0.2 * second), (10, one)]),
        ):
            parts = put(pieces, 16)
            ref[:, lanes] = jnp.concatenate([parts[c[0]] for c in COMBOS], axis=0)
        return carry

    lax.fori_loop(0, source_blocks // WIDE, prepare_sources, 0)
    lax.fori_loop(0, (offset + width - 1) // width, prepare_targets, 0)
    totals[...] = jnp.zeros_like(totals)
    turns = source_count // (tile * unroll)
    tb = TARGET_TILE // LANES

    def cell(step, carry):
        i_at, j_at = step // turns, step % turns
        lanes = pl.ds(pl.multiple_of(i_at * TARGET_TILE, TARGET_TILE), TARGET_TILE)
        xs=[jnp.concatenate([due[i_at * tb + q, k : k + 1, :] for q in range(tb)],axis=1) for k in range(3)]
        sums = [None, None, None]
        for turn in range(unroll):
            js = pl.ds(pl.multiple_of((j_at * unroll + turn) * tile, tile), tile)
            rate = dot(right_rate[js, 0:96], left_rate[:, lanes])
            second = dot(right_second[js, 0:96], left_second[:, lanes])
            spread = None
            for k in range(3):
                there = jnp.concatenate([place[k, js, :]] * tb, axis=1)
                delta = there - xs[k]
                spread = delta * delta + SOFTENING if spread is None else spread + delta * delta
            recip = lax.rsqrt(spread)
            square = recip * recip
            cube = recip * square
            p = rate * square
            weights = (cube, p * cube, (p * p - second * square) * cube)
            for k, weight in enumerate(weights):
                high = weight.astype(BF16)
                low = (weight - high.astype(F32)).astype(BF16)
                feat = feats[32 * k : min(32 * k + 32, 80), js]
                part = dot(feat, high) + dot(feat, low)
                sums[k] = part if sums[k] is None else sums[k] + part
        totals[:, lanes] += jnp.concatenate(sums, axis=0)
        return carry

    lax.fori_loop(0, tiles * turns, cell, 0)

    def finish(block, carry):
        t = totals[:, pl.ds(pl.multiple_of(block * LANES, LANES), LANES)]
        c = t[0:10] + t[10:20] + t[20:30]
        p = t[32:39] + t[39:46] + t[46:53]
        u = t[64:68] + t[68:72] + t[72:76]
        x, v, a = (due[block, k : k + 3, :] for k in (0, 3, 6))
        results[block, 0:3, :] = c[1:4] - x * c[0:1]
        results[block, 3:6, :] = c[4:7] - v * c[0:1] - 3.0 * (p[1:4] - x * p[0:1])
        results[block, 6:9, :] = (
            c[7:10] - a * c[0:1] - 6.0 * (p[4:7] - v * p[0:1]) + 15.0 * (u[1:4] - x * u[0:1])
        )
        return carry

    lax.fori_loop(0, tiles * tb, finish, 0)

    def return_due(block, carry):
        at, shift = offsets[block] // LANES, offsets[block] % LANES
        both = jnp.where(lane >= shift, results[at], results[at + 1])
        out[block] = pltpu.roll(both, (LANES - shift) % LANES, 1)[0:9]
        return carry

    lax.fori_loop(0, target_blocks, return_due, 0)


def pair_sums(targets, sources, tile=256, unroll=8):
    target_count, source_count = targets.shape[0] * LANES, sources.shape[0] * LANES
    return pl.pallas_call(
        functools.partial(pair_kernel, tile, unroll),
        out_shape=jax.ShapeDtypeStruct((targets.shape[0], 9, LANES), F32),
        in_specs=[pl.BlockSpec(memory_space=pltpu.VMEM)] * 2,
        out_specs=pl.BlockSpec(memory_space=pltpu.VMEM),
        scratch_shapes=[
            pltpu.VMEM((80, WIDE * LANES), F32),
            pltpu.VMEM((96, target_count), BF16),
            pltpu.VMEM((96, target_count), BF16),
            pltpu.VMEM((source_count, LANES), BF16),
            pltpu.VMEM((source_count, LANES), BF16),
            pltpu.VMEM((80, source_count), BF16),
            pltpu.VMEM((3, source_count, LANES), F32),
            pltpu.VMEM((80, target_count), F32),
            pltpu.VMEM((targets.shape[0] + 2, 16, LANES), F32),
            pltpu.VMEM((targets.shape[0] + 2, 16, LANES), F32),
            pltpu.SMEM((targets.shape[0],), jnp.int32),
        ],
        compiler_params=pltpu.CompilerParams(vmem_limit_bytes=56 * 2**20),
        name="pair_sums",
    )(targets, sources)


def due_first(mask):
    row = lax.broadcasted_iota(jnp.int32, (LANES, LANES), 0)
    star = lax.broadcasted_iota(jnp.int32, (LANES, LANES), 1)
    ones = jnp.broadcast_to(mask.astype(F32), (16, LANES)).astype(BF16)
    rank = dot(ones, jnp.where(row <= star, 1.0, 0.0).astype(BF16))[0:1]
    count = rank[:, LANES - 1 : LANES]
    index = star[0:1].astype(F32)
    to = jnp.where(mask > 0, rank - 1.0, count + index - rank)
    return jnp.where(jnp.broadcast_to(to, (LANES, LANES)) == row.astype(F32), 1.0, 0.0).astype(BF16)


def moved(value, order, dims):
    parts = split3(value)
    h, m, l = (
        lax.dot_general(parts[k], order, (dims, ((), ())), preferred_element_type=F32) for k in "hml"
    )
    return (h + m) + l


def pack_kernel(phase, mass, mask, plane, line, stage):
    stage[...] = jnp.zeros_like(stage)
    stage[0:9, :] = phase[...]
    stage[9:10, :] = mass[...]
    stage[DUE : DUE + 1, :] = mask[...].astype(F32)
    packed = moved(stage[...], due_first(mask[...]), ((1,), (1,)))
    plane[...] = jnp.broadcast_to(packed[None], plane.shape)
    line[...] = jnp.broadcast_to(packed[None], line.shape)


def unpack_kernel(scale, sums, mask, out, stage):
    stage[...] = jnp.zeros_like(stage)
    stage[0:9, :] = jnp.sum(sums[...], axis=0)
    back = moved(stage[...], due_first(mask[...]), ((1,), (0,)))
    out[...] = back[0:9] * scale * mask[...].astype(F32)


def small_call(kernel, shapes, name, *args):
    vmem = pl.BlockSpec(memory_space=pltpu.VMEM)
    return pl.pallas_call(
        kernel,
        out_shape=tuple(jax.ShapeDtypeStruct(shape, F32) for shape in shapes),
        in_specs=[vmem] * len(args),
        out_specs=(vmem,) * len(shapes),
        scratch_shapes=[pltpu.VMEM((16, LANES), F32)],
        name=name,
    )(*args)


AXES = ("row", "col")


def device_groups(rows, cols):
    planes, lines = {}, {}
    for row in range(rows):
        for col in range(cols):
            z_hi, inner = row // 8, row % 8
            z_lo, x = col // 4, col % 4
            planes.setdefault((z_hi, z_lo), []).append(row * cols + col)
            lines.setdefault((inner, x), []).append(row * cols + col)
    return list(planes.values()), list(lines.values())


def exchange(blocks, groups):
    return lax.all_to_all(blocks, AXES, 0, 0, axis_index_groups=groups, tiled=True)


def on_device(star_phase, star_mass, due_mask):
    rows, cols = lax.axis_size("row"), lax.axis_size("col")
    planes, lines = device_groups(rows, cols)
    mass, mask = star_mass[None, :], due_mask[None, :]
    shapes = [(len(groups[0]), 16, LANES) for groups in (planes, lines)]
    for_plane, for_line = small_call(pack_kernel, shapes, "pack_stars", star_phase, mass, mask)
    targets = exchange(for_plane, planes)
    sources = exchange(for_line, lines)
    sums = exchange(pair_sums(targets, sources), planes)
    scale = 1.0 / (LANES * rows * cols)
    kernel = functools.partial(unpack_kernel, scale)
    return small_call(kernel, [star_phase.shape], "unpack_sums", sums, mask)[0]


def solution(mesh):
    return jax.shard_map(
        on_device, mesh=mesh, in_specs=(P(None, AXES), P(AXES), P(AXES)), out_specs=P(None, AXES), check_vma=False
    )
```

```python
import functools

import jax
import jax.numpy as jnp
from jax import lax
from jax.experimental import pallas as pl
from jax.experimental.pallas import tpu as pltpu
from jax.sharding import PartitionSpec as P

F32 = jnp.float32
BF16 = jnp.bfloat16
SOFTENING = 0.01
LANES = 128
TARGET_TILE = 256
WIDE = 4
DUE = 10
COMBOS = ("hh", "hm", "mh", "mm", "hl", "lh")


def split3(value):
    high = value.astype(BF16)
    rest = value - high.astype(F32)
    middle = rest.astype(BF16)
    low = (rest - middle.astype(F32)).astype(BF16)
    return {"h": high, "m": middle, "l": low}


def dot(left, right):
    return jnp.dot(left, right, preferred_element_type=F32)


def pair_kernel(
    tile, unroll, targets, sources, out, stage, left_rate, left_second,
    right_rate, right_second, feats, place, totals, due, results
):
    target_blocks, source_blocks = targets.shape[0], sources.shape[0]
    target_count, source_count = target_blocks * LANES, source_blocks * LANES
    width = WIDE * LANES

    def rows(ref, block, low, high):
        return jnp.concatenate([ref[block * WIDE + k, low:high, :] for k in range(WIDE)], axis=1)

    def put(pieces, height):
        stage[0:height, :] = jnp.zeros((height, width), F32)
        for at, piece in pieces:
            stage[at : at + piece.shape[0], :] = piece
        return split3(stage[0:height, :])

    one = jnp.ones((1, width), F32)

    def prepare_sources(block, carry):
        lanes = pl.ds(pl.multiple_of(block * width, width), width)
        x, v, a = (rows(sources, block, k, k + 3) for k in (0, 3, 6))
        m = rows(sources, block, 9, 10)
        x_v = jnp.sum(x * v, axis=0, keepdims=True)
        second = jnp.sum(v * v + x * a, axis=0, keepdims=True)
        empty = jnp.zeros((32, width), F32)
        for ref, pieces in (
            (right_rate, [(0, v), (3, x), (6, one), (7, x_v)]),
            (right_second, [(0, 0.2 * v), (3, 0.2 * a), (6, 0.2 * x), (9, one), (10, 0.2 * second)]),
        ):
            parts = put(pieces, 16)
            tall = jnp.concatenate([parts[c[1]].astype(F32) for c in COMBOS] + [empty], axis=0)
            ref[lanes, :] = tall.T.astype(BF16)
        for k in range(3):
            place[k, lanes, :] = jnp.broadcast_to(x[k : k + 1, :], (LANES, width)).T
        parts = put([(0, m), (1, m * x), (4, m * v), (7, m * a)], 16)
        stage[...] = jnp.zeros_like(stage)
        for k, name in enumerate("hml"):
            part = parts[name].astype(F32)
            stage[10 * k : 10 * k + 10, :] = part[0:10]
            stage[32 + 7 * k : 39 + 7 * k, :] = part[0:7]
            stage[64 + 4 * k : 68 + 4 * k, :] = part[0:4]
        feats[:, lanes] = stage[...].astype(BF16)
        return carry

    lane = lax.broadcasted_iota(jnp.int32, (16, LANES), 1)
    counts = [jnp.sum(targets[k, DUE : DUE + 1, :]).astype(jnp.int32) for k in range(target_blocks)]
    starts, offset = [], jnp.int32(0)
    for count in counts:
        starts.append(offset)
        offset = offset + count
    pairs_of_blocks = (offset + LANES - 1) // TARGET_TILE
    odd_block = (offset + LANES - 1) // LANES - 2 * pairs_of_blocks
    due[...] = jnp.zeros_like(due)
    results[...] = jnp.zeros_like(results)

    placed = []
    for k in range(target_blocks):
        at, shift = starts[k] >> 7, starts[k] & (LANES - 1)
        placed.append((at, shift))
        moved_block = pltpu.roll(targets[k], shift, 1)
        due[at] = jnp.where(lane >= shift, moved_block, due[at])
        due[at + 1] = moved_block

    def prepare_targets(block, carry):
        lanes = pl.ds(pl.multiple_of(block * width, width), width)
        x, v, a = (rows(due, block, k, k + 3) for k in (0, 3, 6))
        x_v = jnp.sum(x * v, axis=0, keepdims=True)
        second = jnp.sum(v * v + x * a, axis=0, keepdims=True)
        for ref, pieces in (
            (left_rate, [(0, -x), (3, -v), (6, x_v), (7, one)]),
            (left_second, [(0, -2.0 * v), (3, -x), (6, -a), (9, 0.2 * second), (10, one)]),
        ):
            parts = put(pieces, 16)
            ref[:, lanes] = jnp.concatenate([parts[c[0]] for c in COMBOS], axis=0)
        return carry

    lax.fori_loop(0, source_blocks // WIDE, prepare_sources, 0)
    lax.fori_loop(0, (offset + width - 1) // width, prepare_targets, 0)
    totals[...] = jnp.zeros_like(totals)
    turns = source_count // (tile * unroll)

    def cell(first, tb, j_at):
        lanes = pl.ds(pl.multiple_of(first * LANES, LANES), tb * LANES)
        xs = [
            jnp.concatenate([due[first + q, k : k + 1, :] for q in range(tb)], axis=1)
            for k in range(3)
        ]
        sums = [None, None, None]
        for turn in range(unroll):
            js = pl.ds(pl.multiple_of((j_at * unroll + turn) * tile, tile), tile)
            rate = dot(right_rate[js, 0:96], left_rate[:, lanes])
            second = dot(right_second[js, 0:96], left_second[:, lanes])
            spread = None
            for k in range(3):
                there = jnp.concatenate([place[k, js, :]] * tb, axis=1)
                delta = there - xs[k]
                spread = delta * delta + SOFTENING if spread is None else spread + delta * delta
            recip = lax.rsqrt(spread)
            square = recip * recip
            cube = recip * square
            p = rate * square
            weights = (cube, p * cube, (p * p - second * square) * cube)
            for k, weight in enumerate(weights):
                high = weight.astype(BF16)
                low = (weight - high.astype(F32)).astype(BF16)
                feat = feats[32 * k : min(32 * k + 32, 80), js]
                part = dot(feat, high) + dot(feat, low)
                sums[k] = part if sums[k] is None else sums[k] + part
        totals[:, lanes] += jnp.concatenate(sums, axis=0)

    def wide_cell(step, carry):
        cell(step // turns * 2, 2, step % turns)
        return carry

    def narrow_cell(step, carry):
        cell(pairs_of_blocks * 2, 1, step)
        return carry

    lax.fori_loop(0, pairs_of_blocks * turns, wide_cell, 0)
    lax.fori_loop(0, odd_block * turns, narrow_cell, 0)

    def finish(block, carry):
        t = totals[:, pl.ds(pl.multiple_of(block * LANES, LANES), LANES)]
        c = t[0:10] + t[10:20] + t[20:30]
        p = t[32:39] + t[39:46] + t[46:53]
        u = t[64:68] + t[68:72] + t[72:76]
        x, v, a = (due[block, k : k + 3, :] for k in (0, 3, 6))
        results[block, 0:3, :] = c[1:4] - x * c[0:1]
        results[block, 3:6, :] = c[4:7] - v * c[0:1] - 3.0 * (p[1:4] - x * p[0:1])
        results[block, 6:9, :] = (
            c[7:10] - a * c[0:1] - 6.0 * (p[4:7] - v * p[0:1]) + 15.0 * (u[1:4] - x * u[0:1])
        )
        return carry

    lax.fori_loop(0, pairs_of_blocks * 2 + odd_block, finish, 0)

    for k, (at, shift) in enumerate(placed):
        both = jnp.where(lane >= shift, results[at], results[at + 1])
        out[k] = pltpu.roll(both, (LANES - shift) & (LANES - 1), 1)[0:9]


def pair_sums(targets, sources, tile=256, unroll=8):
    target_count, source_count = targets.shape[0] * LANES, sources.shape[0] * LANES
    return pl.pallas_call(
        functools.partial(pair_kernel, tile, unroll),
        out_shape=jax.ShapeDtypeStruct((targets.shape[0], 9, LANES), F32),
        in_specs=[pl.BlockSpec(memory_space=pltpu.VMEM)] * 2,
        out_specs=pl.BlockSpec(memory_space=pltpu.VMEM),
        scratch_shapes=[
            pltpu.VMEM((80, WIDE * LANES), F32),
            pltpu.VMEM((96, target_count), BF16),
            pltpu.VMEM((96, target_count), BF16),
            pltpu.VMEM((source_count, LANES), BF16),
            pltpu.VMEM((source_count, LANES), BF16),
            pltpu.VMEM((80, source_count), BF16),
            pltpu.VMEM((3, source_count, LANES), F32),
            pltpu.VMEM((80, target_count), F32),
            pltpu.VMEM((targets.shape[0] + 2, 16, LANES), F32),
            pltpu.VMEM((targets.shape[0] + 2, 16, LANES), F32),
        ],
        compiler_params=pltpu.CompilerParams(vmem_limit_bytes=56 * 2**20),
        name="pair_sums",
    )(targets, sources)


def due_first(mask):
    row = lax.broadcasted_iota(jnp.int32, (LANES, LANES), 0)
    star = lax.broadcasted_iota(jnp.int32, (LANES, LANES), 1)
    ones = jnp.broadcast_to(mask.astype(F32), (16, LANES)).astype(BF16)
    rank = dot(ones, jnp.where(row <= star, 1.0, 0.0).astype(BF16))[0:1]
    count = rank[:, LANES - 1 : LANES]
    index = star[0:1].astype(F32)
    to = jnp.where(mask > 0, rank - 1.0, count + index - rank)
    return jnp.where(jnp.broadcast_to(to, (LANES, LANES)) == row.astype(F32), 1.0, 0.0).astype(BF16)


def moved(value, order, dims):
    parts = split3(value)
    h, m, l = (
        lax.dot_general(parts[k], order, (dims, ((), ())), preferred_element_type=F32) for k in "hml"
    )
    return (h + m) + l


def pack_kernel(phase, mass, mask, plane, line, stage):
    stage[...] = jnp.zeros_like(stage)
    stage[0:9, :] = phase[...]
    stage[9:10, :] = mass[...]
    stage[DUE : DUE + 1, :] = mask[...].astype(F32)
    packed = moved(stage[...], due_first(mask[...]), ((1,), (1,)))
    plane[...] = jnp.broadcast_to(packed[None], plane.shape)
    line[...] = jnp.broadcast_to(packed[None], line.shape)


def unpack_kernel(scale, sums, mask, out, stage):
    stage[...] = jnp.zeros_like(stage)
    stage[0:9, :] = jnp.sum(sums[...], axis=0)
    back = moved(stage[...], due_first(mask[...]), ((1,), (0,)))
    out[...] = back[0:9] * scale * mask[...].astype(F32)


def small_call(kernel, shapes, name, *args):
    vmem = pl.BlockSpec(memory_space=pltpu.VMEM)
    return pl.pallas_call(
        kernel,
        out_shape=tuple(jax.ShapeDtypeStruct(shape, F32) for shape in shapes),
        in_specs=[vmem] * len(args),
        out_specs=(vmem,) * len(shapes),
        scratch_shapes=[pltpu.VMEM((16, LANES), F32)],
        name=name,
    )(*args)


AXES = ("row", "col")


def device_groups(rows, cols):
    planes, lines = {}, {}
    for row in range(rows):
        for col in range(cols):
            z_hi, inner = row // 8, row % 8
            z_lo, x = col // 4, col % 4
            planes.setdefault((z_hi, z_lo), []).append(row * cols + col)
            lines.setdefault((inner, x), []).append(row * cols + col)
    return list(planes.values()), list(lines.values())


def exchange(blocks, groups):
    return lax.all_to_all(blocks, AXES, 0, 0, axis_index_groups=groups, tiled=True)


def on_device(star_phase, star_mass, due_mask):
    rows, cols = lax.axis_size("row"), lax.axis_size("col")
    planes, lines = device_groups(rows, cols)
    mass, mask = star_mass[None, :], due_mask[None, :]
    shapes = [(len(groups[0]), 16, LANES) for groups in (planes, lines)]
    for_plane, for_line = small_call(pack_kernel, shapes, "pack_stars", star_phase, mass, mask)
    targets = exchange(for_plane, planes)
    sources = exchange(for_line, lines)
    sums = exchange(pair_sums(targets, sources), planes)
    scale = 1.0 / (LANES * rows * cols)
    kernel = functools.partial(unpack_kernel, scale)
    return small_call(kernel, [star_phase.shape], "unpack_sums", sums, mask)[0]


def solution(mesh):
    return jax.shard_map(
        on_device, mesh=mesh, in_specs=(P(None, AXES), P(AXES), P(AXES)), out_specs=P(None, AXES), check_vma=False
    )
```

```python
import functools

import jax
import jax.numpy as jnp
from jax import lax
from jax.experimental import pallas as pl
from jax.experimental.pallas import tpu as pltpu
from jax.sharding import PartitionSpec as P

F32 = jnp.float32
BF16 = jnp.bfloat16
SOFTENING = 0.01
LANES = 128
TARGET_TILE = 256
WIDE = 4
DUE = 10
COMBOS = ("hh", "hm", "mh", "mm", "hl", "lh")


def split3(value):
    high = value.astype(BF16)
    rest = value - high.astype(F32)
    middle = rest.astype(BF16)
    low = (rest - middle.astype(F32)).astype(BF16)
    return {"h": high, "m": middle, "l": low}


def dot(left, right):
    return jnp.dot(left, right, preferred_element_type=F32)


def rows_of(ref, block, low, high):
    return jnp.concatenate([ref[block * WIDE + k, low:high, :] for k in range(WIDE)], axis=1)


def staged(stage, pieces, height):
    stage[0:height, :] = jnp.zeros((height, stage.shape[1]), F32)
    for at, piece in pieces:
        stage[at : at + piece.shape[0], :] = piece
    return split3(stage[0:height, :])


def target_kernel(targets, due, left_rate, left_second, starts, stage):
    width = WIDE * LANES
    one = jnp.ones((1, width), F32)
    target_blocks = targets.shape[0]
    lane = lax.broadcasted_iota(jnp.int32, (16, LANES), 1)
    counts = [jnp.sum(targets[k, DUE : DUE + 1, :]).astype(jnp.int32) for k in range(target_blocks)]
    offset, begins = jnp.int32(0), []
    for k, count in enumerate(counts):
        begins.append(offset)
        starts[k] = offset
        offset = offset + count
    starts[target_blocks] = offset
    due[...] = jnp.zeros_like(due)

    for k in range(target_blocks):
        at, shift = begins[k] >> 7, begins[k] & (LANES - 1)
        moved_block = pltpu.roll(targets[k], shift, 1)
        due[at] = jnp.where(lane >= shift, moved_block, due[at])
        due[at + 1] = moved_block

    def prepare_targets(block, carry):
        lanes = pl.ds(pl.multiple_of(block * width, width), width)
        x, v, a = (rows_of(due, block, k, k + 3) for k in (0, 3, 6))
        x_v = jnp.sum(x * v, axis=0, keepdims=True)
        second = jnp.sum(v * v + x * a, axis=0, keepdims=True)
        for ref, pieces in (
            (left_rate, [(0, -x), (3, -v), (6, x_v), (7, one)]),
            (left_second, [(0, -2.0 * v), (3, -x), (6, -a), (9, 0.2 * second), (10, one)]),
        ):
            parts = staged(stage, pieces, 16)
            ref[:, lanes] = jnp.concatenate([parts[c[0]] for c in COMBOS], axis=0)
        return carry

    lax.fori_loop(0, (offset + width - 1) // width, prepare_targets, 0)


def pair_kernel(
    tile, unroll, due, left_rate, left_second, starts, sources, out, stage,
    right_rate, right_second, feats, place, totals, results
):
    target_blocks, source_blocks = out.shape[0], sources.shape[0]
    source_count = source_blocks * LANES
    width = WIDE * LANES
    total = starts[target_blocks]
    pairs_of_blocks = (total + LANES - 1) // TARGET_TILE
    odd_block = (total + LANES - 1) // LANES - 2 * pairs_of_blocks
    results[...] = jnp.zeros_like(results)
    one = jnp.ones((1, width), F32)

    def prepare_sources(block, carry):
        lanes = pl.ds(pl.multiple_of(block * width, width), width)
        x, v, a = (rows_of(sources, block, k, k + 3) for k in (0, 3, 6))
        m = rows_of(sources, block, 9, 10)
        x_v = jnp.sum(x * v, axis=0, keepdims=True)
        second = jnp.sum(v * v + x * a, axis=0, keepdims=True)
        empty = jnp.zeros((32, width), F32)
        for ref, pieces in (
            (right_rate, [(0, v), (3, x), (6, one), (7, x_v)]),
            (right_second, [(0, 0.2 * v), (3, 0.2 * a), (6, 0.2 * x), (9, one), (10, 0.2 * second)]),
        ):
            parts = staged(stage, pieces, 16)
            tall = jnp.concatenate([parts[c[1]].astype(F32) for c in COMBOS] + [empty], axis=0)
            ref[lanes, :] = tall.T.astype(BF16)
        for k in range(3):
            place[k, lanes, :] = jnp.broadcast_to(x[k : k + 1, :], (LANES, width)).T
        parts = staged(stage, [(0, m), (1, m * x), (4, m * v), (7, m * a)], 16)
        stage[...] = jnp.zeros_like(stage)
        for k, name in enumerate("hml"):
            part = parts[name].astype(F32)
            stage[10 * k : 10 * k + 10, :] = part[0:10]
            stage[32 + 7 * k : 39 + 7 * k, :] = part[0:7]
            stage[64 + 4 * k : 68 + 4 * k, :] = part[0:4]
        feats[:, lanes] = stage[...].astype(BF16)
        return carry

    lax.fori_loop(0, source_blocks // WIDE, prepare_sources, 0)
    totals[...] = jnp.zeros_like(totals)
    turns = source_count // (tile * unroll)

    def cell(first, tb, j_at):
        lanes = pl.ds(pl.multiple_of(first * LANES, LANES), tb * LANES)
        xs = [
            jnp.concatenate([due[first + q, k : k + 1, :] for q in range(tb)], axis=1)
            for k in range(3)
        ]
        sums = [None, None, None]
        for turn in range(unroll):
            js = pl.ds(pl.multiple_of((j_at * unroll + turn) * tile, tile), tile)
            rate = dot(right_rate[js, 0:96], left_rate[:, lanes])
            second = dot(right_second[js, 0:96], left_second[:, lanes])
            spread = None
            for k in range(3):
                there = jnp.concatenate([place[k, js, :]] * tb, axis=1)
                delta = there - xs[k]
                spread = delta * delta + SOFTENING if spread is None else spread + delta * delta
            recip = lax.rsqrt(spread)
            square = recip * recip
            cube = recip * square
            p = rate * square
            weights = (cube, p * cube, (p * p - second * square) * cube)
            for k, weight in enumerate(weights):
                high = weight.astype(BF16)
                low = (weight - high.astype(F32)).astype(BF16)
                feat = feats[32 * k : min(32 * k + 32, 80), js]
                part = dot(feat, high) + dot(feat, low)
                sums[k] = part if sums[k] is None else sums[k] + part
        totals[:, lanes] += jnp.concatenate(sums, axis=0)

    def wide_cell(step, carry):
        cell(step // turns * 2, 2, step % turns)
        return carry

    def narrow_cell(step, carry):
        cell(pairs_of_blocks * 2, 1, step)
        return carry

    lax.fori_loop(0, pairs_of_blocks * turns, wide_cell, 0)
    lax.fori_loop(0, odd_block * turns, narrow_cell, 0)

    def finish(block, carry):
        t = totals[:, pl.ds(pl.multiple_of(block * LANES, LANES), LANES)]
        c = t[0:10] + t[10:20] + t[20:30]
        p = t[32:39] + t[39:46] + t[46:53]
        u = t[64:68] + t[68:72] + t[72:76]
        x, v, a = (due[block, k : k + 3, :] for k in (0, 3, 6))
        results[block, 0:3, :] = c[1:4] - x * c[0:1]
        results[block, 3:6, :] = c[4:7] - v * c[0:1] - 3.0 * (p[1:4] - x * p[0:1])
        results[block, 6:9, :] = (
            c[7:10] - a * c[0:1] - 6.0 * (p[4:7] - v * p[0:1]) + 15.0 * (u[1:4] - x * u[0:1])
        )
        return carry

    lax.fori_loop(0, pairs_of_blocks * 2 + odd_block, finish, 0)

    lane = lax.broadcasted_iota(jnp.int32, (16, LANES), 1)
    for k in range(target_blocks):
        at, shift = starts[k] >> 7, starts[k] & (LANES - 1)
        both = jnp.where(lane >= shift, results[at], results[at + 1])
        out[k] = pltpu.roll(both, (LANES - shift) & (LANES - 1), 1)[0:9]


def prepared_targets(targets):
    blocks = targets.shape[0]
    in_vmem = pl.BlockSpec(memory_space=pltpu.VMEM)
    return pl.pallas_call(
        target_kernel,
        out_shape=(
            jax.ShapeDtypeStruct((blocks + 2, 16, LANES), F32),
            jax.ShapeDtypeStruct((96, blocks * LANES), BF16),
            jax.ShapeDtypeStruct((96, blocks * LANES), BF16),
            jax.ShapeDtypeStruct((blocks + 1,), jnp.int32),
        ),
        in_specs=[in_vmem],
        out_specs=(in_vmem, in_vmem, in_vmem, pl.BlockSpec(memory_space=pltpu.SMEM)),
        scratch_shapes=[pltpu.VMEM((16, WIDE * LANES), F32)],
        compiler_params=pltpu.CompilerParams(vmem_limit_bytes=16 * 2**20),
        name="prepare_targets",
    )(targets)


def pair_sums(prepared, sources, tile=256, unroll=8):
    target_count, source_count = prepared[1].shape[1], sources.shape[0] * LANES
    target_blocks = target_count // LANES
    in_vmem = pl.BlockSpec(memory_space=pltpu.VMEM)
    return pl.pallas_call(
        functools.partial(pair_kernel, tile, unroll),
        out_shape=jax.ShapeDtypeStruct((target_blocks, 9, LANES), F32),
        in_specs=[in_vmem] * 3 + [pl.BlockSpec(memory_space=pltpu.SMEM), in_vmem],
        out_specs=in_vmem,
        scratch_shapes=[
            pltpu.VMEM((80, WIDE * LANES), F32),
            pltpu.VMEM((source_count, LANES), BF16),
            pltpu.VMEM((source_count, LANES), BF16),
            pltpu.VMEM((80, source_count), BF16),
            pltpu.VMEM((3, source_count, LANES), F32),
            pltpu.VMEM((80, target_count), F32),
            pltpu.VMEM((target_blocks + 2, 16, LANES), F32),
        ],
        compiler_params=pltpu.CompilerParams(vmem_limit_bytes=24 * 2**20),
        name="pair_sums",
    )(*prepared, sources)


def due_first(mask):
    row = lax.broadcasted_iota(jnp.int32, (LANES, LANES), 0)
    star = lax.broadcasted_iota(jnp.int32, (LANES, LANES), 1)
    ones = jnp.broadcast_to(mask.astype(F32), (16, LANES)).astype(BF16)
    rank = dot(ones, jnp.where(row <= star, 1.0, 0.0).astype(BF16))[0:1]
    count = rank[:, LANES - 1 : LANES]
    index = star[0:1].astype(F32)
    to = jnp.where(mask > 0, rank - 1.0, count + index - rank)
    return jnp.where(jnp.broadcast_to(to, (LANES, LANES)) == row.astype(F32), 1.0, 0.0).astype(BF16)


def moved(value, order, dims):
    parts = split3(value)
    h, m, l = (
        lax.dot_general(parts[k], order, (dims, ((), ())), preferred_element_type=F32) for k in "hml"
    )
    return (h + m) + l


def pack_kernel(phase, mass, mask, copies, stage):
    stage[...] = jnp.zeros_like(stage)
    stage[0:9, :] = phase[...]
    stage[9:10, :] = mass[...]
    stage[DUE : DUE + 1, :] = mask[...].astype(F32)
    packed = moved(stage[...], due_first(mask[...]), ((1,), (1,)))
    copies[...] = jnp.broadcast_to(packed[None], copies.shape)


def unpack_kernel(scale, sums, mask, out, stage):
    stage[...] = jnp.zeros_like(stage)
    stage[0:9, :] = jnp.sum(sums[...], axis=0)
    back = moved(stage[...], due_first(mask[...]), ((1,), (0,)))
    out[...] = back[0:9] * scale * mask[...].astype(F32)


def small_call(kernel, shapes, name, *args):
    vmem = pl.BlockSpec(memory_space=pltpu.VMEM)
    return pl.pallas_call(
        kernel,
        out_shape=tuple(jax.ShapeDtypeStruct(shape, F32) for shape in shapes),
        in_specs=[vmem] * len(args),
        out_specs=(vmem,) * len(shapes),
        scratch_shapes=[pltpu.VMEM((16, LANES), F32)],
        name=name,
    )(*args)


AXES = ("row", "col")


def device_groups(rows, cols):
    planes, lines = {}, {}
    for row in range(rows):
        for col in range(cols):
            z_hi, inner = row // 8, row % 8
            z_lo, x = col // 4, col % 4
            planes.setdefault((z_hi, z_lo), []).append(row * cols + col)
            lines.setdefault((inner, x), []).append(row * cols + col)
    return list(planes.values()), list(lines.values())


def exchange(blocks, groups):
    return lax.all_to_all(blocks, AXES, 0, 0, axis_index_groups=groups, tiled=True)


def on_device(star_phase, star_mass, due_mask):
    rows, cols = lax.axis_size("row"), lax.axis_size("col")
    planes, lines = device_groups(rows, cols)
    mass, mask = star_mass[None, :], due_mask[None, :]
    packed = [
        small_call(pack_kernel, [(len(groups[0]), 16, LANES)], name, star_phase, mass, mask)[0]
        for groups, name in ((planes, "pack_plane"), (lines, "pack_line"))
    ]
    targets = exchange(packed[0], planes)
    sources = exchange(packed[1], lines)
    sums = exchange(pair_sums(prepared_targets(targets), sources), planes)
    scale = 1.0 / (LANES * rows * cols)
    kernel = functools.partial(unpack_kernel, scale)
    return small_call(kernel, [star_phase.shape], "unpack_sums", sums, mask)[0]


def solution(mesh):
    return jax.shard_map(
        on_device, mesh=mesh, in_specs=(P(None, AXES), P(AXES), P(AXES)), out_specs=P(None, AXES), check_vma=False
    )
```

```python
import functools

import jax
import jax.numpy as jnp
from jax import lax
from jax.experimental import pallas as pl
from jax.experimental.pallas import tpu as pltpu
from jax.sharding import PartitionSpec as P

F32 = jnp.float32
BF16 = jnp.bfloat16
SOFTENING = 0.01
LANES = 128
TARGET_TILE = 256
WIDE = 4
DUE = 10
COMBOS = ("hh", "hm", "mh", "mm", "hl", "lh")


def split3(value):
    high = value.astype(BF16)
    rest = value - high.astype(F32)
    middle = rest.astype(BF16)
    low = (rest - middle.astype(F32)).astype(BF16)
    return {"h": high, "m": middle, "l": low}


def dot(left, right):
    return jnp.dot(left, right, preferred_element_type=F32)


def rows_of(ref, block, low, high):
    return jnp.concatenate([ref[block * WIDE + k, low:high, :] for k in range(WIDE)], axis=1)


def staged(stage, pieces, height):
    stage[0:height, :] = jnp.zeros((height, stage.shape[1]), F32)
    for at, piece in pieces:
        stage[at : at + piece.shape[0], :] = piece
    return split3(stage[0:height, :])


def target_kernel(targets, due, left_rate, left_second, starts, stage):
    width = WIDE * LANES
    one = jnp.ones((1, width), F32)
    target_blocks = targets.shape[0]
    lane = lax.broadcasted_iota(jnp.int32, (16, LANES), 1)
    counts = [jnp.sum(targets[k, DUE : DUE + 1, :]).astype(jnp.int32) for k in range(target_blocks)]
    offset, begins = jnp.int32(0), []
    for k, count in enumerate(counts):
        begins.append(offset)
        starts[k] = offset
        offset = offset + count
    starts[target_blocks] = offset
    due[...] = jnp.zeros_like(due)

    for k in range(target_blocks):
        at, shift = begins[k] >> 7, begins[k] & (LANES - 1)
        moved_block = pltpu.roll(targets[k], shift, 1)
        due[at] = jnp.where(lane >= shift, moved_block, due[at])
        due[at + 1] = moved_block

    def prepare_targets(block, carry):
        lanes = pl.ds(pl.multiple_of(block * width, width), width)
        x, v, a = (rows_of(due, block, k, k + 3) for k in (0, 3, 6))
        x_v = jnp.sum(x * v, axis=0, keepdims=True)
        second = jnp.sum(v * v + x * a, axis=0, keepdims=True)
        for ref, pieces in (
            (left_rate, [(0, -x), (3, -v), (6, x_v), (7, one)]),
            (left_second, [(0, -2.0 * v), (3, -x), (6, -a), (9, 0.2 * second), (10, one)]),
        ):
            parts = staged(stage, pieces, 16)
            ref[:, lanes] = jnp.concatenate([parts[c[0]] for c in COMBOS], axis=0)
        return carry

    lax.fori_loop(0, (offset + width - 1) // width, prepare_targets, 0)


def pair_kernel(
    tile, unroll, due, left_rate, left_second, starts, sources, out, stage,
    right_rate, right_second, feats, place, totals, results
):
    target_blocks, source_blocks = out.shape[0], sources.shape[0]
    source_count = source_blocks * LANES
    width = WIDE * LANES
    total = starts[target_blocks]
    pairs_of_blocks = (total + LANES - 1) // TARGET_TILE
    odd_block = (total + LANES - 1) // LANES - 2 * pairs_of_blocks
    results[...] = jnp.zeros_like(results)
    one = jnp.ones((1, width), F32)

    def prepare_sources(block, carry):
        lanes = pl.ds(pl.multiple_of(block * width, width), width)
        x, v, a = (rows_of(sources, block, k, k + 3) for k in (0, 3, 6))
        m = rows_of(sources, block, 9, 10)
        x_v = jnp.sum(x * v, axis=0, keepdims=True)
        second = jnp.sum(v * v + x * a, axis=0, keepdims=True)
        empty = jnp.zeros((32, width), F32)
        for ref, pieces in (
            (right_rate, [(0, v), (3, x), (6, one), (7, x_v)]),
            (right_second, [(0, 0.2 * v), (3, 0.2 * a), (6, 0.2 * x), (9, one), (10, 0.2 * second)]),
        ):
            parts = staged(stage, pieces, 16)
            tall = jnp.concatenate([parts[c[1]].astype(F32) for c in COMBOS] + [empty], axis=0)
            ref[lanes, :] = tall.T.astype(BF16)
        for k in range(3):
            place[k, lanes, :] = jnp.broadcast_to(x[k : k + 1, :], (LANES, width)).T
        parts = staged(stage, [(0, m), (1, m * x), (4, m * v), (7, m * a)], 16)
        stage[...] = jnp.zeros_like(stage)
        for k, name in enumerate("hml"):
            part = parts[name].astype(F32)
            stage[10 * k : 10 * k + 10, :] = part[0:10]
            stage[32 + 7 * k : 39 + 7 * k, :] = part[0:7]
            stage[64 + 4 * k : 68 + 4 * k, :] = part[0:4]
        feats[:, lanes] = stage[...].astype(BF16)
        return carry

    lax.fori_loop(0, source_blocks // WIDE, prepare_sources, 0, unroll=True)
    totals[...] = jnp.zeros_like(totals)
    turns = source_count // (tile * unroll)

    def cell(first, tb, j_at):
        lanes = pl.ds(pl.multiple_of(first * LANES, LANES), tb * LANES)
        xs = [
            jnp.concatenate([due[first + q, k : k + 1, :] for q in range(tb)], axis=1)
            for k in range(3)
        ]
        sums = [None, None, None]
        for turn in range(unroll):
            js = pl.ds(pl.multiple_of((j_at * unroll + turn) * tile, tile), tile)
            rate = dot(right_rate[js, 0:96], left_rate[:, lanes])
            second = dot(right_second[js, 0:96], left_second[:, lanes])
            spread = None
            for k in range(3):
                there = jnp.concatenate([place[k, js, :]] * tb, axis=1)
                delta = there - xs[k]
                spread = delta * delta + SOFTENING if spread is None else spread + delta * delta
            recip = lax.rsqrt(spread)
            square = recip * recip
            cube = recip * square
            p = rate * square
            weights = (cube, p * cube, (p * p - second * square) * cube)
            for k, weight in enumerate(weights):
                high = weight.astype(BF16)
                low = (weight - high.astype(F32)).astype(BF16)
                feat = feats[32 * k : min(32 * k + 32, 80), js]
                part = dot(feat, high) + dot(feat, low)
                sums[k] = part if sums[k] is None else sums[k] + part
        totals[:, lanes] += jnp.concatenate(sums, axis=0)

    def wide_cell(step, carry):
        cell(step // turns * 2, 2, step % turns)
        return carry

    def narrow_cell(step, carry):
        cell(pairs_of_blocks * 2, 1, step)
        return carry

    lax.fori_loop(0, pairs_of_blocks * turns, wide_cell, 0)
    lax.fori_loop(0, odd_block * turns, narrow_cell, 0)

    def finish(block, carry):
        t = totals[:, pl.ds(pl.multiple_of(block * LANES, LANES), LANES)]
        c = t[0:10] + t[10:20] + t[20:30]
        p = t[32:39] + t[39:46] + t[46:53]
        u = t[64:68] + t[68:72] + t[72:76]
        x, v, a = (due[block, k : k + 3, :] for k in (0, 3, 6))
        results[block, 0:3, :] = c[1:4] - x * c[0:1]
        results[block, 3:6, :] = c[4:7] - v * c[0:1] - 3.0 * (p[1:4] - x * p[0:1])
        results[block, 6:9, :] = (
            c[7:10] - a * c[0:1] - 6.0 * (p[4:7] - v * p[0:1]) + 15.0 * (u[1:4] - x * u[0:1])
        )
        return carry

    lax.fori_loop(0, target_blocks, finish, 0, unroll=True)

    lane = lax.broadcasted_iota(jnp.int32, (16, LANES), 1)
    for k in range(target_blocks):
        at, shift = starts[k] >> 7, starts[k] & (LANES - 1)
        both = jnp.where(lane >= shift, results[at], results[at + 1])
        out[k] = pltpu.roll(both, (LANES - shift) & (LANES - 1), 1)[0:9]


def prepared_targets(targets):
    blocks = targets.shape[0]
    in_vmem = pl.BlockSpec(memory_space=pltpu.VMEM)
    return pl.pallas_call(
        target_kernel,
        out_shape=(
            jax.ShapeDtypeStruct((blocks + 2, 16, LANES), F32),
            jax.ShapeDtypeStruct((96, blocks * LANES), BF16),
            jax.ShapeDtypeStruct((96, blocks * LANES), BF16),
            jax.ShapeDtypeStruct((blocks + 1,), jnp.int32),
        ),
        in_specs=[in_vmem],
        out_specs=(in_vmem, in_vmem, in_vmem, pl.BlockSpec(memory_space=pltpu.SMEM)),
        scratch_shapes=[pltpu.VMEM((16, WIDE * LANES), F32)],
        compiler_params=pltpu.CompilerParams(vmem_limit_bytes=16 * 2**20),
        name="prepare_targets",
    )(targets)


def pair_sums(prepared, sources, tile=256, unroll=8):
    target_count, source_count = prepared[1].shape[1], sources.shape[0] * LANES
    target_blocks = target_count // LANES
    in_vmem = pl.BlockSpec(memory_space=pltpu.VMEM)
    return pl.pallas_call(
        functools.partial(pair_kernel, tile, unroll),
        out_shape=jax.ShapeDtypeStruct((target_blocks, 9, LANES), F32),
        in_specs=[in_vmem] * 3 + [pl.BlockSpec(memory_space=pltpu.SMEM), in_vmem],
        out_specs=in_vmem,
        scratch_shapes=[
            pltpu.VMEM((80, WIDE * LANES), F32),
            pltpu.VMEM((source_count, LANES), BF16),
            pltpu.VMEM((source_count, LANES), BF16),
            pltpu.VMEM((80, source_count), BF16),
            pltpu.VMEM((3, source_count, LANES), F32),
            pltpu.VMEM((80, target_count), F32),
            pltpu.VMEM((target_blocks + 2, 16, LANES), F32),
        ],
        compiler_params=pltpu.CompilerParams(vmem_limit_bytes=24 * 2**20),
        name="pair_sums",
    )(*prepared, sources)


def due_first(mask):
    row = lax.broadcasted_iota(jnp.int32, (LANES, LANES), 0)
    star = lax.broadcasted_iota(jnp.int32, (LANES, LANES), 1)
    ones = jnp.broadcast_to(mask.astype(F32), (16, LANES)).astype(BF16)
    rank = dot(ones, jnp.where(row <= star, 1.0, 0.0).astype(BF16))[0:1]
    count = rank[:, LANES - 1 : LANES]
    index = star[0:1].astype(F32)
    to = jnp.where(mask > 0, rank - 1.0, count + index - rank)
    return jnp.where(jnp.broadcast_to(to, (LANES, LANES)) == row.astype(F32), 1.0, 0.0).astype(BF16)


def moved(value, order, dims):
    parts = split3(value)
    h, m, l = (
        lax.dot_general(parts[k], order, (dims, ((), ())), preferred_element_type=F32) for k in "hml"
    )
    return (h + m) + l


def pack_kernel(phase, mass, mask, copies, stage):
    stage[...] = jnp.zeros_like(stage)
    stage[0:9, :] = phase[...]
    stage[9:10, :] = mass[...]
    stage[DUE : DUE + 1, :] = mask[...].astype(F32)
    packed = moved(stage[...], due_first(mask[...]), ((1,), (1,)))
    copies[...] = jnp.broadcast_to(packed[None], copies.shape)


def unpack_kernel(scale, sums, mask, out, stage):
    stage[...] = jnp.zeros_like(stage)
    stage[0:9, :] = jnp.sum(sums[...], axis=0)
    back = moved(stage[...], due_first(mask[...]), ((1,), (0,)))
    out[...] = back[0:9] * scale * mask[...].astype(F32)


def small_call(kernel, shapes, name, *args):
    vmem = pl.BlockSpec(memory_space=pltpu.VMEM)
    return pl.pallas_call(
        kernel,
        out_shape=tuple(jax.ShapeDtypeStruct(shape, F32) for shape in shapes),
        in_specs=[vmem] * len(args),
        out_specs=(vmem,) * len(shapes),
        scratch_shapes=[pltpu.VMEM((16, LANES), F32)],
        name=name,
    )(*args)


AXES = ("row", "col")


def device_groups(rows, cols):
    planes, lines = {}, {}
    for row in range(rows):
        for col in range(cols):
            z_hi, inner = row // 8, row % 8
            z_lo, x = col // 4, col % 4
            planes.setdefault((z_hi, z_lo), []).append(row * cols + col)
            lines.setdefault((inner, x), []).append(row * cols + col)
    return list(planes.values()), list(lines.values())


def exchange(blocks, groups):
    return lax.all_to_all(blocks, AXES, 0, 0, axis_index_groups=groups, tiled=True)


def on_device(star_phase, star_mass, due_mask):
    rows, cols = lax.axis_size("row"), lax.axis_size("col")
    planes, lines = device_groups(rows, cols)
    mass, mask = star_mass[None, :], due_mask[None, :]
    packed = [
        small_call(pack_kernel, [(len(groups[0]), 16, LANES)], name, star_phase, mass, mask)[0]
        for groups, name in ((planes, "pack_plane"), (lines, "pack_line"))
    ]
    targets = exchange(packed[0], planes)
    sources = exchange(packed[1], lines)
    sums = exchange(pair_sums(prepared_targets(targets), sources), planes)
    scale = 1.0 / (LANES * rows * cols)
    kernel = functools.partial(unpack_kernel, scale)
    return small_call(kernel, [star_phase.shape], "unpack_sums", sums, mask)[0]


def solution(mesh):
    return jax.shard_map(
        on_device, mesh=mesh, in_specs=(P(None, AXES), P(AXES), P(AXES)), out_specs=P(None, AXES), check_vma=False
    )
```
